128 devices in a mesh: frame: 16 (over x_hi, z, core), head: 8 (over y, x_lo).
Axes of the slice: x: 4 (x_hi: 2, x_lo: 2; x = x_hi * 2 + x_lo), y: 4, z: 4, core: 2. Of those that a mesh axis runs over, the one named last changes fastest.
Arguments:
- latents: bfloat16 [64, 128, 5120], P('frame'), may hold values from -6 to 6
- levels: int32 [64], P('frame'), may hold values from 0 to 49
- mod_table: float32 [50, 3, 5120], replicated, may hold values from -3 to 3
- w_query: bfloat16 [5120, 3072], P(None, 'head')
- w_key: bfloat16 [5120, 3072], P(None, 'head')
- w_value: bfloat16 [5120, 3072], P(None, 'head'), may hold values from -0.078125 to 0.078125
- w_out: bfloat16 [3072, 5120], P('head'), may hold values from -0.109375 to 0.109375
- query_gain: float32 [3072], P('head'), may hold values from 0.5 to 5
- key_gain: float32 [3072], P('head'), may hold values from 0.5 to 5
Outputs:
- advanced: bfloat16 [64, 128, 5120], P('frame', None, 'head')
The draws below stay inside these ranges and needn't reach their ends.
All inputs are finite; a program needn't handle non-finite values.
Results may differ from the reference program's by a relative error of at most 0.0055.
Values may be sent and summed in bfloat16 or wider, within the bound.
A program may use at most 128 MiB of HBM per device.

```python
import jax
import jax.numpy as jnp
from jax import lax

D = 5120
HS = 128
HEADS = 24
FR_DEV = 4
P_SIZE = 128
LEVELS = 50
FRAMES = 64


def query_columns(key):
    column_key = jax.random.fold_in(key, 7)
    return jax.random.truncated_normal(column_key, -6.0, 6.0, (D, HEADS * HS), jnp.float32) * D ** (-0.5)


def draw_w_query(key, part):
    return query_columns(key).astype(jnp.bfloat16)


def draw_w_key(key, part):
    key = jax.random.fold_in(key, 5)
    own = jax.random.truncated_normal(key, -6.0, 6.0, (D, HEADS * HS), jnp.float32) * D ** (-0.5)
    return own.astype(jnp.bfloat16)


def draw_query_gain(key, part):
    key = jax.random.fold_in(key, 11)
    return jax.random.uniform(key, (HEADS * HS,), jnp.float32, 0.5, 2.5)


def draw_key_gain(key, part):
    key = jax.random.fold_in(key, 23)
    return jax.random.uniform(key, (HEADS * HS,), jnp.float32, 0.5, 2.5)


def draw_mod_table(key, part):
    key = jax.random.fold_in(key, 41)
    return 0.5 * jax.random.truncated_normal(key, -6.0, 6.0, (LEVELS, 3, D), jnp.float32)


def draw_latents(key, part):
    key = jax.random.fold_in(key, 53)
    base = jax.random.truncated_normal(key, -6.0, 6.0, (FRAMES, P_SIZE, D), jnp.float32)
    return base.astype(jnp.bfloat16)


def place_ends(entries, key, low, high):
    spot = [jax.random.randint(jax.random.fold_in(key, axis), (), 0, length) for axis, length in enumerate(entries.shape)]
    widest = entries.shape.index(max(entries.shape))
    next_to = spot[:widest] + [(spot[widest] + 1) % entries.shape[widest]] + spot[widest + 1:]
    return entries.at[tuple(spot)].set(low).at[tuple(next_to)].set(high)


def shard_levels(key, extent, pieces, smallest, high):
    def one(dim, shards_of):
        heights = jax.random.uniform(jax.random.fold_in(jax.random.fold_in(key, 6), dim), (shards_of,), jnp.float32, smallest / len(pieces), high / len(pieces))
        return jnp.repeat(jnp.exp(heights), extent[dim] // shards_of).reshape((-1,) + (1,) * (len(extent) - dim - 1))

    factor_of = one(*pieces[0])
    for cut in pieces[1:]:
        factor_of = factor_of * one(*cut)
    return factor_of


def normal_values(own_key, dims, scale, limit, shards=(), kind=jnp.bfloat16):
    values = jax.random.normal(own_key, dims, jnp.float32) * scale
    if len(shards) > 0:
        values = shard_levels(own_key, dims, shards, -0.22, 0.18) * values
    return jnp.clip(values, min=-limit, max=limit).astype(kind)


def setup_inputs(seed: int = 0) -> dict:
    arg_keys = jax.random.split(jax.random.key(seed), 10)
    latents = draw_latents(jax.random.fold_in(arg_keys[9], 71), 0)
    levels = place_ends(jax.random.randint(arg_keys[1], (FRAMES,), 0, LEVELS), jax.random.fold_in(arg_keys[1], 1), 0, LEVELS - 1).astype(jnp.int32)
    mod_table = draw_mod_table(jax.random.fold_in(arg_keys[9], 71), 0)
    w_query = draw_w_query(jax.random.fold_in(arg_keys[9], 71), 0)
    w_key = draw_w_key(jax.random.fold_in(arg_keys[9], 71), 0)
    w_value = normal_values(arg_keys[5], (D, HEADS * HS), D ** -0.5, 0.078125, ((1, 8),))
    w_out = normal_values(arg_keys[6], (HEADS * HS, D), (HEADS * HS) ** -0.5, 0.109375, ((0, 8),))
    query_gain = draw_query_gain(jax.random.fold_in(arg_keys[9], 71), 0)
    key_gain = draw_key_gain(jax.random.fold_in(arg_keys[9], 71), 0)
    return dict(latents=latents, levels=levels, mod_table=mod_table, w_query=w_query, w_key=w_key, w_value=w_value, w_out=w_out, query_gain=query_gain, key_gain=key_gain)


def head_norm(projected, gain):
    shaped = projected.reshape(projected.shape[0], projected.shape[1], HEADS, HS)
    power = lax.optimization_barrier(jnp.mean(shaped * shaped, axis=-1, keepdims=True))
    normed = shaped * lax.rsqrt(power + 1e-06) * gain.reshape(HEADS, HS)
    return normed.astype(jnp.bfloat16)

def reference(latents, levels, mod_table, w_query, w_key, w_value, w_out, query_gain, key_gain):
    modulation = mod_table[levels]
    source = latents.astype(jnp.float32)
    average = lax.optimization_barrier(jnp.mean(source, axis=-1, keepdims=True))
    centred = source - average
    variance = lax.optimization_barrier(jnp.mean(centred * centred, axis=-1, keepdims=True))
    normed = centred * lax.rsqrt(variance + 1e-06)
    hidden = (normed * (1.0 + modulation[:, 1][:, None, :]) + modulation[:, 0][:, None, :]).astype(jnp.bfloat16)
    flat = hidden.reshape(FRAMES * P_SIZE, D)
    queries = head_norm(jnp.dot(flat, w_query, preferred_element_type=jnp.float32).reshape(FRAMES, P_SIZE, HEADS * HS), query_gain)
    key_rows = head_norm(jnp.dot(flat, w_key, preferred_element_type=jnp.float32).reshape(FRAMES, P_SIZE, HEADS * HS), key_gain)
    value_rows = jnp.dot(flat, w_value, preferred_element_type=jnp.float32).astype(jnp.bfloat16).reshape(FRAMES, P_SIZE, HEADS, HS)
    scores = jnp.einsum('fphd,gphd->phfg', queries.astype(jnp.float32), key_rows.astype(jnp.float32)) * (1.0 / HS ** 0.5)
    largest = lax.optimization_barrier(jnp.max(scores, axis=-1, keepdims=True))
    powers = jnp.exp(scores - largest)
    totals = lax.optimization_barrier(jnp.sum(powers, axis=-1))
    rounded = powers.astype(jnp.bfloat16)
    numerator = jnp.einsum('phfg,gphd->fphd', rounded.astype(jnp.float32), value_rows.astype(jnp.float32))
    attended = (numerator / jnp.transpose(totals, (2, 0, 1))[..., None]).astype(jnp.bfloat16)
    projected = jnp.dot(attended.reshape(FRAMES * P_SIZE, HEADS * HS), w_out, preferred_element_type=jnp.float32).reshape(FRAMES, P_SIZE, D)
    block_out = (source + modulation[:, 2][:, None, :] * projected).astype(jnp.bfloat16)
    return jnp.roll(block_out, FR_DEV, axis=0)
```

```python
import functools

import jax
import jax.numpy as jnp
from jax import lax
from jax.experimental import pallas as pl
from jax.experimental.pallas import tpu as pltpu
from jax.sharding import PartitionSpec as P

HS = 128
EPS = 1e-06
MESH = pl.DeviceIdType.MESH
BF16, F32 = jnp.bfloat16, jnp.float32


def block_kernel(
    slots,
    ys,
    levels_ref,
    latents_hbm,
    table_hbm,
    wq_hbm,
    wk_hbm,
    wv_hbm,
    wo_hbm,
    qgain_ref,
    kgain_ref,
    out_ref,
    lat,
    table,
    modrows,
    hidden,
    weights,
    sent,
    got,
    attended,
    gathered,
    wout,
    psend,
    precv,
    pown,
    residual,
    gate_out,
    gate_in,
    load_sem,
    in_send,
    in_recv,
    back_send,
    back_recv,
    y_send,
    y_recv,
    w_send,
    w_recv,
    sib_send,
    sib_recv,
    x_send,
    x_recv,
    shift_send,
    shift_recv,
):
    frames, positions, width = lat.shape
    cols = sent.shape[2]
    heads = cols // HS
    rows = frames * positions
    chunk = rows // slots
    out_cols = width // (2 * ys)
    quarter = rows // 4
    me = lax.axis_index("frame")
    head = lax.axis_index("head")
    y, xlo = head // 2, head % 2
    core = me % 2
    sibling = me + 1 - 2 * core
    following = (me + 1) % slots
    half = cols // 2

    lat_parts = 4
    part = positions // lat_parts
    lat_loads = [
        pltpu.make_async_copy(
            latents_hbm.at[:, pl.ds(q * part, part), :],
            lat.at[:, pl.ds(q * part, part), :],
            load_sem.at[q],
        )
        for q in range(lat_parts)
    ]
    table_load = pltpu.make_async_copy(table_hbm, table, load_sem.at[4])
    weight_loads = [
        pltpu.make_async_copy(w_hbm, weights.at[t], load_sem.at[5 + t])
        for t, w_hbm in enumerate((wk_hbm, wv_hbm, wq_hbm))
    ]
    table_load.start()
    for load in lat_loads:
        load.start()
    for load in weight_loads:
        load.start()

    barrier = pltpu.get_barrier_semaphore()

    def greet(k, carry):
        pl.semaphore_signal(
            barrier, inc=1, device_id=((me + k) % slots, head), device_id_type=MESH
        )
        return carry

    lax.fori_loop(1, slots, greet, 0)
    for k in range(1, ys):
        pl.semaphore_signal(
            barrier, inc=1, device_id=(me, ((y + k) % ys) * 2 + xlo), device_id_type=MESH
        )
    pl.semaphore_signal(barrier, inc=1, device_id=(me, y * 2 + 1 - xlo), device_id_type=MESH)
    pl.semaphore_wait(barrier, slots - 1 + ys - 1 + 1)

    w_rows = pl.ds(pl.multiple_of(core * half, 64), half)
    w_copies = []
    for k in (1, ys - 1) + tuple(range(2, ys - 1)):
        peer = (y + k) % ys
        for s in range(2):
            copy = pltpu.make_async_remote_copy(
                src_ref=wo_hbm.at[w_rows, pl.ds(pl.multiple_of((peer * 2 + s) * out_cols, 128), out_cols)],
                dst_ref=wout.at[s, pl.ds(pl.multiple_of(y * cols + core * half, 64), half), :],
                send_sem=w_send.at[k - 1, s],
                recv_sem=w_recv.at[k - 1, s],
                device_id=(me, peer * 2 + xlo),
                device_id_type=MESH,
            )
            copy.start()
            w_copies.append((k, s, copy))
    own_w = []
    for s in range(2):
        copy = pltpu.make_async_copy(
            wo_hbm.at[:, pl.ds(pl.multiple_of((y * 2 + s) * out_cols, 128), out_cols)],
            wout.at[s, pl.ds(pl.multiple_of(y * cols, 128), cols), :],
            load_sem.at[8 + s],
        )
        copy.start()
        own_w.append(copy)

    table_load.wait()
    head_cols = pl.ds(pl.multiple_of(head * out_cols, 128), out_cols)
    for f in range(frames):
        level = levels_ref[f]
        modrows[f, 0] = jnp.broadcast_to(1.0 + table[level, 1:2, :], (8, width))
        modrows[f, 1] = jnp.broadcast_to(table[level, 0:1, :], (8, width))
        gate_out[f] = jnp.broadcast_to(table[level, 2:3, head_cols], (8, out_cols))

    shift_copies = [
        pltpu.make_async_remote_copy(
            src_ref=src,
            dst_ref=dst,
            send_sem=shift_send.at[n],
            recv_sem=shift_recv.at[n],
            device_id=(following, head),
            device_id_type=MESH,
        )
        for n, (src, dst) in enumerate(
            ((gate_out, gate_in), (latents_hbm.at[:, :, head_cols], residual))
        )
    ]

    step = 512

    def normalise(j, carry):
        low, high = [], []
        at = pl.ds(pl.multiple_of(j * 16, 16), 16)
        stats = []
        for f in range(frames):
            total = jnp.zeros((16, 128), F32)
            for c in range(0, width, 128):
                total += lat[f, at, c : c + 128].astype(F32)
            mean = jnp.sum(total, axis=-1, keepdims=True) * (1.0 / width)
            square = jnp.zeros((16, 128), F32)
            for c in range(0, width, 128):
                centred = lat[f, at, c : c + 128].astype(F32) - mean
                square += centred * centred
            var = jnp.sum(square, axis=-1, keepdims=True) * (1.0 / width)
            stats.append((mean, lax.rsqrt(var + EPS)))
        for c in range(0, width, step):
            at_c = slice(c, c + step)
            pieces = []
            for f in range(frames):
                mean, rstd = stats[f]
                scale = modrows[f, 0, :, at_c]
                offset = modrows[f, 1, :, at_c]
                normed = (lat[f, at, at_c].astype(F32) - mean) * rstd
                pieces.append((normed[:8] * scale + offset, normed[8:] * scale + offset))
            for side in range(2):
                for pair in range(frames // 2):
                    both = jnp.concatenate(
                        [pieces[2 * pair][side], pieces[2 * pair + 1][side]], axis=0
                    )
                    start = pl.multiple_of(j * 64 + side * 32 + pair * 16, 16)
                    hidden[pl.ds(start, 16), at_c] = both.astype(BF16)
        return carry

    per_part = part // 16
    for q in range(lat_parts):
        lat_loads[q].wait()
        lax.fori_loop(q * per_part, (q + 1) * per_part, normalise, 0)

    in_local = []
    for t in range(3):
        weight_loads[t].wait()
        projected = jnp.dot(hidden[...], weights[t], preferred_element_type=F32)
        for n in range(heads):
            at_n = slice(n * HS, (n + 1) * HS)
            one = projected[:, at_n]
            if t != 1:
                gain = (qgain_ref if t == 2 else kgain_ref)[:, at_n]
                power = jnp.mean(one * one, axis=-1, keepdims=True)
                one = one * lax.rsqrt(power + EPS) * gain
            sent[t, :, at_n] = one.astype(BF16)

        def send(k, carry):
            to = (me + k) % slots
            pltpu.make_async_remote_copy(
                src_ref=sent.at[t, pl.ds(pl.multiple_of(to * chunk, 32), chunk), :],
                dst_ref=got.at[t, pl.ds(pl.multiple_of(me * chunk, 32), chunk), :],
                send_sem=in_send.at[t],
                recv_sem=in_recv.at[t],
                device_id=(to, head),
                device_id_type=MESH,
            ).start()
            return carry

        lax.fori_loop(1, slots, send, 0)
        own = pl.ds(pl.multiple_of(me * chunk, 32), chunk)
        copy = pltpu.make_async_copy(sent.at[t, own, :], got.at[t, own, :], load_sem.at[10 + t])
        copy.start()
        in_local.append(copy)

    for copy in shift_copies:
        copy.start()

    for t in range(3):
        in_local[t].wait()
        others = got.at[t, pl.ds(0, rows - chunk), :]
        pltpu.make_async_copy(others, others, in_recv.at[t]).wait()

    per_slot = positions // slots
    row_at = lax.broadcasted_iota(jnp.int32, (per_slot, rows), 0)
    col_at = lax.broadcasted_iota(jnp.int32, (per_slot, rows), 1)
    bias = jnp.where(row_at == col_at % per_slot, 0.0, -1e9).astype(F32)
    q_rows = 256
    for n in range(heads):
        at_n = slice(n * HS, (n + 1) * HS)
        keys = got[0, :, at_n]
        values = jnp.concatenate([got[1, :, at_n], jnp.ones((rows, HS), BF16)], axis=1)
        for b in range(rows // q_rows):
            at_b = slice(b * q_rows, (b + 1) * q_rows)
            scores = lax.dot_general(
                got[2, at_b, at_n], keys, (((1,), (1,)), ((), ())), preferred_element_type=F32
            )
            scores = scores.reshape(q_rows // per_slot, per_slot, rows) + bias[None]
            largest = jnp.max(scores, axis=-1, keepdims=True)
            powers = jnp.exp((scores - largest) * (1.0 / HS**0.5))
            mixed = jnp.dot(
                powers.reshape(q_rows, rows).astype(BF16), values, preferred_element_type=F32
            )
            attended[at_b, at_n] = (mixed[:, :HS] / mixed[:, HS:]).astype(BF16)

    own_cols = pl.ds(pl.multiple_of(y * cols, 128), cols)
    arrive = gathered.at[pl.ds(pl.multiple_of(me * chunk, 32), chunk), own_cols]

    def send_back(k, carry):
        to = (me + k) % slots
        owner = (me + k + slots - 1) % slots
        pltpu.make_async_remote_copy(
            src_ref=attended.at[pl.ds(pl.multiple_of(owner * chunk, 32), chunk), :],
            dst_ref=arrive,
            send_sem=back_send,
            recv_sem=back_recv.at[me // (slots // 4)],
            device_id=(to, head),
            device_id_type=MESH,
        ).start()
        return carry

    lax.fori_loop(1, slots, send_back, 0)
    before = (me + slots - 1) % slots
    pltpu.make_async_copy(
        attended.at[pl.ds(pl.multiple_of(before * chunk, 32), chunk), :],
        arrive,
        back_recv.at[me // (slots // 4)],
    ).start()

    sib_copies = []
    for k, s, copy in w_copies:
        copy.wait()
        source = (y + ys - k) % ys
        piece = wout.at[s, pl.ds(pl.multiple_of(source * cols + core * half, 64), half), :]
        forward = pltpu.make_async_remote_copy(
            src_ref=piece,
            dst_ref=piece,
            send_sem=sib_send.at[k - 1, s],
            recv_sem=sib_recv.at[k - 1, s],
            device_id=(sibling, head),
            device_id_type=MESH,
        )
        forward.start()
        sib_copies.append(forward)

    y_copies = []
    for r in range(4):
        piece = gathered.at[pl.ds(r * quarter, quarter), own_cols]
        pltpu.make_async_copy(piece, piece, back_recv.at[r]).wait()
        for k in (1, ys - 1) + tuple(range(2, ys - 1)):
            copy = pltpu.make_async_remote_copy(
                src_ref=piece,
                dst_ref=piece,
                send_sem=y_send.at[r, k - 1],
                recv_sem=y_recv.at[r, k - 1],
                device_id=(me, ((y + k) % ys) * 2 + xlo),
                device_id_type=MESH,
            )
            copy.start()
            y_copies.append(copy)

    for copy in own_w + sib_copies:
        copy.wait()

    x_copies = []
    for r in range(4):
        at_r = slice(r * quarter, (r + 1) * quarter)
        for copy in y_copies[r * (ys - 1) : (r + 1) * (ys - 1)]:
            copy.wait()
        mixed = gathered[at_r, :]
        psend[at_r, :] = jnp.dot(mixed, wout[1 - xlo], preferred_element_type=F32).astype(BF16)
        copy = pltpu.make_async_remote_copy(
            src_ref=psend.at[pl.ds(r * quarter, quarter), :],
            dst_ref=precv.at[pl.ds(r * quarter, quarter), :],
            send_sem=x_send.at[r],
            recv_sem=x_recv.at[r],
            device_id=(me, y * 2 + 1 - xlo),
            device_id_type=MESH,
        )
        copy.start()
        x_copies.append(copy)
        pown[at_r, :] = jnp.dot(mixed, wout[xlo], preferred_element_type=F32)

    for copy in shift_copies:
        copy.wait()
    for r in range(4):
        x_copies[r].wait()
        for j in range(r * quarter // 64, (r + 1) * quarter // 64):
            at = slice(j * 16, (j + 1) * 16)
            total = pown[j * 64 : (j + 1) * 64, :] + precv[j * 64 : (j + 1) * 64, :].astype(F32)
            for f in range(frames):
                gate = gate_in[f]
                moved = jnp.concatenate(
                    [
                        total[f * 8 : (f + 1) * 8] * gate,
                        total[32 + f * 8 : 32 + (f + 1) * 8] * gate,
                    ],
                    axis=0,
                )
                out_ref[f, at, :] = (residual[f, at, :].astype(F32) + moved).astype(BF16)

    for t in range(3):
        others = sent.at[t, pl.ds(0, rows - chunk), :]
        pltpu.make_async_copy(others, others, in_send.at[t]).wait()
    others = attended.at[pl.ds(0, rows - chunk), :]
    pltpu.make_async_copy(others, others, back_send).wait()


def on_device(slots, ys, latents, levels, mod_table, wq, wk, wv, wo, qgain, kgain):
    frames, positions, width = latents.shape
    cols = wq.shape[1]
    rows = frames * positions
    out_cols = width // (2 * ys)
    vmem = pl.BlockSpec(memory_space=pltpu.VMEM)
    hbm = pl.BlockSpec(memory_space=pl.ANY)
    dma = pltpu.SemaphoreType.DMA
    return pl.pallas_call(
        functools.partial(block_kernel, slots, ys),
        out_shape=jax.ShapeDtypeStruct((frames, positions, out_cols), BF16),
        in_specs=[pl.BlockSpec(memory_space=pltpu.SMEM)] + [hbm] * 6 + [vmem] * 2,
        out_specs=vmem,
        scratch_shapes=[
            pltpu.VMEM((frames, positions, width), BF16),
            pltpu.VMEM(mod_table.shape, F32),
            pltpu.VMEM((frames, 2, 8, width), F32),
            pltpu.VMEM((rows, width), BF16),
            pltpu.VMEM((3, width, cols), BF16),
            pltpu.VMEM((3, rows, cols), BF16),
            pltpu.VMEM((3, rows, cols), BF16),
            pltpu.VMEM((rows, cols), BF16),
            pltpu.VMEM((rows, ys * cols), BF16),
            pltpu.VMEM((2, ys * cols, out_cols), BF16),
            pltpu.VMEM((rows, out_cols), BF16),
            pltpu.VMEM((rows, out_cols), BF16),
            pltpu.VMEM((rows, out_cols), F32),
            pltpu.VMEM((frames, positions, out_cols), BF16),
            pltpu.VMEM((frames, 8, out_cols), F32),
            pltpu.VMEM((frames, 8, out_cols), F32),
            dma((13,)),
            dma((3,)),
            dma((3,)),
            dma(()),
            dma((4,)),
            dma((4, ys - 1)),
            dma((4, ys - 1)),
            dma((ys - 1, 2)),
            dma((ys - 1, 2)),
            dma((ys - 1, 2)),
            dma((ys - 1, 2)),
            dma((4,)),
            dma((4,)),
            dma((2,)),
            dma((2,)),
        ],
        compiler_params=pltpu.CompilerParams(
            collective_id=0, has_side_effects=True, vmem_limit_bytes=60 << 20
        ),
        name="temporal_block",
    )(levels, latents, mod_table, wq, wk, wv, wo, qgain.reshape(1, cols), kgain.reshape(1, cols))


def solution(mesh):
    return jax.shard_map(
        functools.partial(on_device, mesh.shape["frame"], mesh.shape["head"] // 2),
        mesh=mesh,
        in_specs=(
            P("frame", None, None),
            P("frame"),
            P(),
            P(None, "head"),
            P(None, "head"),
            P(None, "head"),
            P("head", None),
            P("head"),
            P("head"),
        ),
        out_specs=P("frame", None, "head"),
        check_vma=False,
    )
```

```python
import functools

import jax
import jax.numpy as jnp
from jax import lax
from jax.experimental import pallas as pl
from jax.experimental.pallas import tpu as pltpu
from jax.sharding import PartitionSpec as P

HS = 128
EPS = 1e-06
MESH = pl.DeviceIdType.MESH
BF16, F32 = jnp.bfloat16, jnp.float32


def swap_halves(first, second):
    upper = lax.broadcasted_iota(jnp.int32, first.shape, 0) < 4
    return (
        jnp.where(upper, first, pltpu.roll(second, 4, 0)),
        jnp.where(upper, pltpu.roll(first, 4, 0), second),
    )


def block_kernel(
    slots,
    ys,
    levels_ref,
    latents_hbm,
    table_hbm,
    wq_hbm,
    wk_hbm,
    wv_hbm,
    wo_hbm,
    qgain_ref,
    kgain_ref,
    out_ref,
    lat,
    table,
    modrows,
    hidden,
    weights,
    sent,
    got,
    attended,
    gathered,
    wout,
    psend,
    precv,
    pown,
    residual,
    gate_out,
    gate_in,
    load_sem,
    in_send,
    in_recv,
    back_send,
    back_recv,
    y_send,
    y_recv,
    w_send,
    w_recv,
    sib_send,
    sib_recv,
    x_send,
    x_recv,
    shift_send,
    shift_recv,
):
    frames, positions, width = lat.shape
    cols = attended.shape[1]
    heads = cols // HS
    rows = frames * positions
    side = rows // 2
    chunk = side // slots
    out_cols = width // (2 * ys)
    quarter = rows // 4
    me = lax.axis_index("frame")
    head = lax.axis_index("head")
    y, xlo = head // 2, head % 2
    core = me % 2
    sibling = me + 1 - 2 * core
    following = (me + 1) % slots
    half = cols // 2

    def ring(steps):
        return (me, ((y + steps) % ys) * 2 + xlo)

    lat_parts = 4
    part = positions // lat_parts
    lat_loads = [
        pltpu.make_async_copy(
            latents_hbm.at[:, pl.ds(q * part, part), :],
            lat.at[:, pl.ds(q * part, part), :],
            load_sem.at[q],
        )
        for q in range(lat_parts)
    ]
    table_load = pltpu.make_async_copy(table_hbm, table, load_sem.at[4])
    weight_loads = [
        pltpu.make_async_copy(w_hbm, weights.at[t], load_sem.at[5 + t])
        for t, w_hbm in enumerate((wk_hbm, wv_hbm, wq_hbm))
    ]
    table_load.start()
    for load in lat_loads:
        load.start()

    barrier = pltpu.get_barrier_semaphore()

    def greet(k, carry):
        pl.semaphore_signal(
            barrier, inc=1, device_id=((me + k) % slots, head), device_id_type=MESH
        )
        return carry

    lax.fori_loop(1, slots, greet, 0)
    for k in range(1, ys):
        pl.semaphore_signal(barrier, inc=1, device_id=ring(k), device_id_type=MESH)
    pl.semaphore_signal(barrier, inc=1, device_id=(me, y * 2 + 1 - xlo), device_id_type=MESH)

    table_load.wait()
    head_cols = pl.ds(pl.multiple_of(head * out_cols, 128), out_cols)
    for f in range(frames):
        level = levels_ref[f]
        modrows[f, 0] = jnp.broadcast_to(1.0 + table[1, pl.ds(level, 1), :], (8, width))
        modrows[f, 1] = jnp.broadcast_to(table[0, pl.ds(level, 1), :], (8, width))
        gate_out[f] = jnp.broadcast_to(table[2, pl.ds(level, 1), head_cols], (8, out_cols))

    pl.semaphore_wait(barrier, slots - 1 + ys - 1 + 1)

    w_rows = pl.ds(pl.multiple_of(core * half, 64), half)
    w_copies = []
    for k in (2, 1, 3):
        peer = (y + k) % ys
        copy = pltpu.make_async_remote_copy(
            src_ref=wo_hbm.at[w_rows, pl.ds(pl.multiple_of(peer * 2 * out_cols, 128), 2 * out_cols)],
            dst_ref=wout.at[pl.ds(pl.multiple_of(y * cols + core * half, 64), half), :],
            send_sem=w_send.at[k - 1],
            recv_sem=w_recv.at[k - 1],
            device_id=ring(k),
            device_id_type=MESH,
        )
        copy.start()
        w_copies.append((k, copy))

    shift_copies = [
        pltpu.make_async_remote_copy(
            src_ref=src,
            dst_ref=dst,
            send_sem=shift_send.at[n],
            recv_sem=shift_recv.at[n],
            device_id=(following, head),
            device_id_type=MESH,
        )
        for n, (src, dst) in enumerate(
            ((gate_out, gate_in), (latents_hbm.at[:, :, head_cols], residual))
        )
    ]
    for copy in shift_copies:
        copy.start()
    for load in weight_loads:
        load.start()
    own_w = pltpu.make_async_copy(
        wo_hbm.at[:, pl.ds(pl.multiple_of(y * 2 * out_cols, 128), 2 * out_cols)],
        wout.at[pl.ds(pl.multiple_of(y * cols, 128), cols), :],
        load_sem.at[8],
    )
    own_w.start()

    step = 512

    def normalise(j, carry):
        at = pl.ds(pl.multiple_of(j * 16, 16), 16)
        stats = []
        for f in range(frames):
            total = jnp.zeros((16, 128), F32)
            for c in range(0, width, 128):
                total += lat[f, at, c : c + 128].astype(F32)
            mean = jnp.sum(total, axis=-1, keepdims=True) * (1.0 / width)
            square = jnp.zeros((16, 128), F32)
            for c in range(0, width, 128):
                centred = lat[f, at, c : c + 128].astype(F32) - mean
                square += centred * centred
            var = jnp.sum(square, axis=-1, keepdims=True) * (1.0 / width)
            stats.append((mean, lax.rsqrt(var + EPS)))
        for c in range(0, width, step):
            at_c = slice(c, c + step)
            pieces = []
            for f in range(frames):
                mean, rstd = stats[f]
                scale = modrows[f, 0, :, at_c]
                offset = modrows[f, 1, :, at_c]
                normed = (lat[f, at, at_c].astype(F32) - mean) * rstd
                pieces.append((normed[:8] * scale + offset, normed[8:] * scale + offset))
            for v in range(2):
                one = swap_halves(pieces[0][v], pieces[1][v])
                two = swap_halves(pieces[2][v], pieces[3][v])
                for s in range(2):
                    both = jnp.concatenate([one[s], two[s]], axis=0)
                    start = pl.multiple_of(j * 64 + v * 32 + s * 16, 16)
                    hidden[pl.ds(start, 16), at_c] = both.astype(BF16)
        return carry

    zs = slots // 4
    xhi, z = me // (2 * zs), (me // 2) % zs
    partners = []
    for across, along in ((1, 2), (0, 1), (1, 1), (0, 3), (1, 3), (0, 2), (1, 0)):
        chip = ((xhi + across) % 2) * 2 * zs + ((z + along) % zs) * 2
        partners += [chip + core, chip + 1 - core]
    partners.append(sibling)

    blocks = [(t, n) for t in range(3) for n in range(heads)]
    pairs = [blocks[b : b + 2] for b in range(0, len(blocks), 2)]
    sends = {0: (0, 2), 2: (2, 6), 4: (6, 9)}
    own = pl.ds(pl.multiple_of(me * chunk, 16), chunk)
    in_local = []

    def project(a):
        at_a = slice(a * side, (a + 1) * side)
        for b, pair in enumerate(pairs):
            if a == 0:
                for t, n in pair:
                    if n == 0:
                        weight_loads[t].wait()
            weight = jnp.concatenate(
                [weights[t, :, n * HS : (n + 1) * HS] for t, n in pair], axis=1
            )
            projected = jnp.dot(hidden[at_a, :], weight, preferred_element_type=F32)
            for m, (t, n) in enumerate(pair):
                one = projected[:, m * HS : (m + 1) * HS]
                if t != 1:
                    gain = (qgain_ref if t == 2 else kgain_ref)[n * HS : (n + 1) * HS]
                    power = jnp.mean(one * one, axis=-1, keepdims=True)
                    one = one * lax.rsqrt(power + EPS) * gain.reshape(1, HS)
                place = (t * heads + n) * HS
                sent[a, :, place : place + HS] = one.astype(BF16)
            if b in sends:
                first, last = sends[b]
                at_s = pl.ds(first * HS, (last - first) * HS)
                for to in partners:
                    pltpu.make_async_remote_copy(
                        src_ref=sent.at[a, pl.ds(pl.multiple_of(to * chunk, 16), chunk), at_s],
                        dst_ref=got.at[a, own, at_s],
                        send_sem=in_send.at[a],
                        recv_sem=in_recv.at[a],
                        device_id=(to, head),
                        device_id_type=MESH,
                    ).start()
        copy = pltpu.make_async_copy(sent.at[a, own, :], got.at[a, own, :], load_sem.at[9 + a])
        copy.start()
        in_local.append(copy)

    per_part = part // 16
    for a in range(2):
        for q in (2 * a, 2 * a + 1):
            lat_loads[q].wait()
            lax.fori_loop(q * per_part, (q + 1) * per_part, normalise, 0)
        project(a)

    per_slot = positions // slots // 2
    row_at = lax.broadcasted_iota(jnp.int32, (8, side), 0)
    col_at = lax.broadcasted_iota(jnp.int32, (8, side), 1)
    bias = jnp.where(row_at % per_slot == col_at % per_slot, 0.0, -1e9).astype(F32)
    own_cols = pl.ds(pl.multiple_of(y * cols, 128), cols)
    before = (me + slots - 1) % slots

    def attend(a):
        in_local[a].wait()
        others = got.at[a, pl.ds(0, side - chunk), :]
        pltpu.make_async_copy(others, others, in_recv.at[a]).wait()
        for n in range(heads):
            keys, values, queries = (
                got[a, :, (t * heads + n) * HS : (t * heads + n + 1) * HS] for t in range(3)
            )
            values = jnp.concatenate([values, jnp.ones((side, HS), BF16)], axis=1)
            scores = lax.dot_general(
                queries, keys, (((1,), (1,)), ((), ())), preferred_element_type=F32
            )
            scores = scores.reshape(side // 8, 8, side) + bias[None]
            largest = jnp.max(scores, axis=-1, keepdims=True)
            powers = jnp.exp((scores - largest) * (1.0 / HS**0.5))
            mixed = jnp.dot(
                powers.reshape(side, side).astype(BF16), values, preferred_element_type=F32
            )
            attended[a * side : (a + 1) * side, n * HS : (n + 1) * HS] = (
                mixed[:, :HS] / mixed[:, HS:]
            ).astype(BF16)

        arrive = gathered.at[pl.ds(pl.multiple_of(a * side + me * chunk, 16), chunk), own_cols]
        sem = back_recv.at[a * 2 + me // (slots // 2)]
        for to in partners:
            owner = (to + slots - 1) % slots
            pltpu.make_async_remote_copy(
                src_ref=attended.at[pl.ds(pl.multiple_of(a * side + owner * chunk, 16), chunk), :],
                dst_ref=arrive,
                send_sem=back_send.at[a],
                recv_sem=sem,
                device_id=(to, head),
                device_id_type=MESH,
            ).start()
        pltpu.make_async_copy(
            attended.at[pl.ds(pl.multiple_of(a * side + before * chunk, 16), chunk), :],
            arrive,
            sem,
        ).start()

    def y_copy(r, kind, steps, source, start, count):
        piece = gathered.at[
            pl.ds(r * quarter + start, count), pl.ds(pl.multiple_of(source * cols, 128), cols)
        ]
        copy = pltpu.make_async_remote_copy(
            src_ref=piece,
            dst_ref=piece,
            send_sem=y_send.at[r, kind],
            recv_sem=y_recv.at[r, kind],
            device_id=ring(steps),
            device_id_type=MESH,
        )
        copy.start()
        return copy

    y_first, y_second = {}, {}

    def spread(r):
        piece = gathered.at[pl.ds(r * quarter, quarter), own_cols]
        pltpu.make_async_copy(piece, piece, back_recv.at[r]).wait()
        y_first[r] = (y_copy(r, 0, 1, y, 0, quarter), y_copy(r, 1, ys - 1, y, 0, quarter))

    def forward(r):
        low, high = y_first[r]
        low.wait()
        one = y_copy(r, 2, 1, (y + ys - 1) % ys, 0, quarter // 2)
        high.wait()
        two = y_copy(r, 3, ys - 1, (y + 1) % ys, quarter // 2, quarter // 2)
        y_second[r] = (one, two)

    x_copies = []

    def combine(r):
        at_r = slice(r * quarter, (r + 1) * quarter)
        for copy in y_second[r]:
            copy.wait()
        partial = jnp.dot(gathered[at_r, :], wout[...], preferred_element_type=F32)
        lower, upper = partial[:, :out_cols], partial[:, out_cols:]
        psend[at_r, :] = jnp.where(xlo == 0, upper, lower).astype(BF16)
        copy = pltpu.make_async_remote_copy(
            src_ref=psend.at[pl.ds(r * quarter, quarter), :],
            dst_ref=precv.at[pl.ds(r * quarter, quarter), :],
            send_sem=x_send.at[r],
            recv_sem=x_recv.at[r],
            device_id=(me, y * 2 + 1 - xlo),
            device_id_type=MESH,
        )
        copy.start()
        x_copies.append(copy)
        pown[at_r, :] = jnp.where(xlo == 0, lower, upper)

    def finish(r):
        x_copies[r].wait()
        for j in range(r * quarter // 64, (r + 1) * quarter // 64):
            at = slice(j * 16, (j + 1) * 16)
            total = pown[j * 64 : (j + 1) * 64, :] + precv[j * 64 : (j + 1) * 64, :].astype(F32)
            moved = [[None, None] for _ in range(frames)]
            for v in range(2):
                for u in range(2):
                    start = v * 32 + u * 8
                    moved[2 * u][v], moved[2 * u + 1][v] = swap_halves(
                        total[start : start + 8], total[start + 16 : start + 24]
                    )
            for f in range(frames):
                added = jnp.concatenate([moved[f][0] * gate_in[f], moved[f][1] * gate_in[f]], axis=0)
                out_ref[f, at, :] = (residual[f, at, :].astype(F32) + added).astype(BF16)

    attend(0)
    spread(0)
    spread(1)
    attend(1)

    sib_copies = []
    for k, copy in w_copies:
        copy.wait()
        source = (y + ys - k) % ys
        piece = wout.at[pl.ds(pl.multiple_of(source * cols + core * half, 64), half), :]
        passed = pltpu.make_async_remote_copy(
            src_ref=piece,
            dst_ref=piece,
            send_sem=sib_send.at[k - 1],
            recv_sem=sib_recv.at[k - 1],
            device_id=(sibling, head),
            device_id_type=MESH,
        )
        passed.start()
        sib_copies.append(passed)

    forward(0)
    forward(1)
    spread(2)
    spread(3)
    for copy in [own_w] + sib_copies:
        copy.wait()
    combine(0)
    forward(2)
    combine(1)
    forward(3)
    combine(2)
    combine(3)
    for copy in shift_copies:
        copy.wait()
    for r in range(4):
        finish(r)

    for a in range(2):
        others = sent.at[a, pl.ds(0, side - chunk), :]
        pltpu.make_async_copy(others, others, in_send.at[a]).wait()
        others = attended.at[pl.ds(0, side - chunk), :]
        pltpu.make_async_copy(others, others, back_send.at[a]).wait()


def on_device(slots, ys, latents, levels, mod_table, wq, wk, wv, wo, qgain, kgain):
    frames, positions, width = latents.shape
    cols = wq.shape[1]
    rows = frames * positions
    out_cols = width // (2 * ys)
    vmem = pl.BlockSpec(memory_space=pltpu.VMEM)
    hbm = pl.BlockSpec(memory_space=pl.ANY)
    dma = pltpu.SemaphoreType.DMA
    return pl.pallas_call(
        functools.partial(block_kernel, slots, ys),
        out_shape=jax.ShapeDtypeStruct((frames, positions, out_cols), BF16),
        in_specs=[pl.BlockSpec(memory_space=pltpu.SMEM)] + [hbm] * 6 + [vmem] * 2,
        out_specs=vmem,
        scratch_shapes=[
            pltpu.VMEM((frames, positions, width), BF16),
            pltpu.VMEM((3, mod_table.shape[0], width), F32),
            pltpu.VMEM((frames, 2, 8, width), F32),
            pltpu.VMEM((rows, width), BF16),
            pltpu.VMEM((3, width, cols), BF16),
            pltpu.VMEM((2, rows // 2, 3 * cols), BF16),
            pltpu.VMEM((2, rows // 2, 3 * cols), BF16),
            pltpu.VMEM((rows, cols), BF16),
            pltpu.VMEM((rows, ys * cols), BF16),
            pltpu.VMEM((ys * cols, 2 * out_cols), BF16),
            pltpu.VMEM((rows, out_cols), BF16),
            pltpu.VMEM((rows, out_cols), BF16),
            pltpu.VMEM((rows, out_cols), F32),
            pltpu.VMEM((frames, positions, out_cols), BF16),
            pltpu.VMEM((frames, 8, out_cols), F32),
            pltpu.VMEM((frames, 8, out_cols), F32),
            dma((11,)),
            dma((2,)),
            dma((2,)),
            dma((2,)),
            dma((4,)),
            dma((4, 4)),
            dma((4, 4)),
            dma((ys - 1,)),
            dma((ys - 1,)),
            dma((ys - 1,)),
            dma((ys - 1,)),
            dma((4,)),
            dma((4,)),
            dma((2,)),
            dma((2,)),
        ],
        compiler_params=pltpu.CompilerParams(
            collective_id=0, has_side_effects=True, vmem_limit_bytes=60 << 20
        ),
        name="temporal_block",
    )(levels, latents, jnp.transpose(mod_table, (1, 0, 2)), wq, wk, wv, wo, qgain, kgain)


def solution(mesh):
    return jax.shard_map(
        functools.partial(on_device, mesh.shape["frame"], mesh.shape["head"] // 2),
        mesh=mesh,
        in_specs=(
            P("frame", None, None),
            P("frame"),
            P(),
            P(None, "head"),
            P(None, "head"),
            P(None, "head"),
            P("head", None),
            P("head"),
            P("head"),
        ),
        out_specs=P("frame", None, "head"),
        check_vma=False,
    )
```

```python
import functools

import jax
import jax.numpy as jnp
from jax import lax
from jax.experimental import pallas as pl
from jax.experimental.pallas import tpu as pltpu
from jax.sharding import PartitionSpec as P

HS = 128
EPS = 1e-06
MESH = pl.DeviceIdType.MESH
BF16, F32 = jnp.bfloat16, jnp.float32


def swap_halves(first, second):
    upper = lax.broadcasted_iota(jnp.int32, first.shape, 0) < 4
    return (
        jnp.where(upper, first, pltpu.roll(second, 4, 0)),
        jnp.where(upper, pltpu.roll(first, 4, 0), second),
    )


def block_kernel(
    slots,
    ys,
    levels_ref,
    latents_hbm,
    table_hbm,
    wq_hbm,
    wk_hbm,
    wv_hbm,
    wo_hbm,
    qgain_ref,
    kgain_ref,
    out_ref,
    lat,
    table,
    modrows,
    hidden,
    weights,
    sent,
    got,
    attended,
    gathered,
    wout,
    psend,
    precv,
    pown,
    residual,
    gate_out,
    gate_in,
    load_sem,
    in_send,
    in_recv,
    back_send,
    back_recv,
    y_send,
    y_recv,
    w_send,
    w_recv,
    sib_send,
    sib_recv,
    x_send,
    x_recv,
    shift_send,
    shift_recv,
):
    frames, positions, width = lat.shape
    cols = attended.shape[1]
    heads = cols // HS
    rows = frames * positions
    side = rows // 2
    chunk = side // slots
    out_cols = width // (2 * ys)
    quarter = rows // 4
    me = lax.axis_index("frame")
    head = lax.axis_index("head")
    y, xlo = head // 2, head % 2
    core = me % 2
    sibling = me + 1 - 2 * core
    following = (me + 1) % slots
    half = cols // 2

    def ring(steps):
        return (me, ((y + steps) % ys) * 2 + xlo)

    lat_parts = 4
    part = positions // lat_parts
    lat_loads = [
        pltpu.make_async_copy(
            latents_hbm.at[:, pl.ds(q * part, part), :],
            lat.at[:, pl.ds(q * part, part), :],
            load_sem.at[q],
        )
        for q in range(lat_parts)
    ]
    table_load = pltpu.make_async_copy(table_hbm, table, load_sem.at[4])
    weight_loads = [
        pltpu.make_async_copy(w_hbm, weights.at[t], load_sem.at[5 + t])
        for t, w_hbm in enumerate((wk_hbm, wv_hbm, wq_hbm))
    ]
    table_load.start()
    for load in lat_loads:
        load.start()

    barrier = pltpu.get_barrier_semaphore()

    def greet(k, carry):
        pl.semaphore_signal(
            barrier, inc=1, device_id=((me + k) % slots, head), device_id_type=MESH
        )
        return carry

    lax.fori_loop(1, slots, greet, 0)
    for k in range(1, ys):
        pl.semaphore_signal(barrier, inc=1, device_id=ring(k), device_id_type=MESH)
    pl.semaphore_signal(barrier, inc=1, device_id=(me, y * 2 + 1 - xlo), device_id_type=MESH)

    table_load.wait()
    head_cols = pl.ds(pl.multiple_of(head * out_cols, 128), out_cols)
    for f in range(frames):
        level = levels_ref[f]
        modrows[f, 0] = jnp.broadcast_to(1.0 + table[1, pl.ds(level, 1), :], (8, width))
        modrows[f, 1] = jnp.broadcast_to(table[0, pl.ds(level, 1), :], (8, width))
        gate_out[f] = jnp.broadcast_to(table[2, pl.ds(level, 1), head_cols], (8, out_cols))

    pl.semaphore_wait(barrier, slots - 1 + ys - 1 + 1)

    w_rows = pl.ds(pl.multiple_of(core * half, 64), half)
    w_copies = []
    for k in (2, 1, 3):
        peer = (y + k) % ys
        copy = pltpu.make_async_remote_copy(
            src_ref=wo_hbm.at[w_rows, pl.ds(pl.multiple_of(peer * 2 * out_cols, 128), 2 * out_cols)],
            dst_ref=wout.at[pl.ds(pl.multiple_of(y * cols + core * half, 64), half), :],
            send_sem=w_send.at[k - 1],
            recv_sem=w_recv.at[k - 1],
            device_id=ring(k),
            device_id_type=MESH,
        )
        copy.start()
        w_copies.append((k, copy))

    shift_copies = [
        pltpu.make_async_remote_copy(
            src_ref=src,
            dst_ref=dst,
            send_sem=shift_send.at[n],
            recv_sem=shift_recv.at[n],
            device_id=(following, head),
            device_id_type=MESH,
        )
        for n, (src, dst) in enumerate(
            ((gate_out, gate_in), (latents_hbm.at[:, :, head_cols], residual))
        )
    ]
    for copy in shift_copies:
        copy.start()
    for load in weight_loads:
        load.start()
    own_w = pltpu.make_async_copy(
        wo_hbm.at[:, pl.ds(pl.multiple_of(y * 2 * out_cols, 128), 2 * out_cols)],
        wout.at[pl.ds(pl.multiple_of(y * cols, 128), cols), :],
        load_sem.at[8],
    )
    own_w.start()

    step = 512

    def normalise(j, carry):
        at = pl.ds(pl.multiple_of(j * 16, 16), 16)
        stats = []
        for f in range(frames):
            total = jnp.zeros((16, 128), F32)
            for c in range(0, width, 128):
                total += lat[f, at, c : c + 128].astype(F32)
            mean = jnp.sum(total, axis=-1, keepdims=True) * (1.0 / width)
            square = jnp.zeros((16, 128), F32)
            for c in range(0, width, 128):
                centred = lat[f, at, c : c + 128].astype(F32) - mean
                square += centred * centred
            var = jnp.sum(square, axis=-1, keepdims=True) * (1.0 / width)
            stats.append((mean, lax.rsqrt(var + EPS)))
        for c in range(0, width, step):
            at_c = slice(c, c + step)
            pieces = []
            for f in range(frames):
                mean, rstd = stats[f]
                scale = modrows[f, 0, :, at_c]
                offset = modrows[f, 1, :, at_c]
                normed = (lat[f, at, at_c].astype(F32) - mean) * rstd
                pieces.append((normed[:8] * scale + offset, normed[8:] * scale + offset))
            for v in range(2):
                one = swap_halves(pieces[0][v], pieces[1][v])
                two = swap_halves(pieces[2][v], pieces[3][v])
                for s in range(2):
                    both = jnp.concatenate([one[s], two[s]], axis=0)
                    start = pl.multiple_of(j * 64 + v * 32 + s * 16, 16)
                    hidden[pl.ds(start, 16), at_c] = both.astype(BF16)
        return carry

    zs = slots // 4
    xhi, z = me // (2 * zs), (me // 2) % zs
    partners = []
    for across, along in ((1, 2), (1, 1), (1, 3), (1, 0), (0, 2), (0, 1), (0, 3)):
        chip = ((xhi + across) % 2) * 2 * zs + ((z + along) % zs) * 2
        partners += [chip + core, chip + 1 - core]
    partners.append(sibling)

    blocks = [(t, n) for t in range(3) for n in range(heads)]
    pairs = [blocks[b : b + 2] for b in range(0, len(blocks), 2)]
    sends = {0: (0, 2), 2: (2, 6), 4: (6, 9)}
    own = pl.ds(pl.multiple_of(me * chunk, 16), chunk)
    in_local = []

    def project(a):
        at_a = slice(a * side, (a + 1) * side)
        for b, pair in enumerate(pairs):
            if a == 0:
                for t, n in pair:
                    if n == 0:
                        weight_loads[t].wait()
            weight = jnp.concatenate(
                [weights[t, :, n * HS : (n + 1) * HS] for t, n in pair], axis=1
            )
            projected = jnp.dot(hidden[at_a, :], weight, preferred_element_type=F32)
            for m, (t, n) in enumerate(pair):
                one = projected[:, m * HS : (m + 1) * HS]
                if t != 1:
                    gain = (qgain_ref if t == 2 else kgain_ref)[n * HS : (n + 1) * HS]
                    power = jnp.mean(one * one, axis=-1, keepdims=True)
                    one = one * lax.rsqrt(power + EPS) * gain.reshape(1, HS)
                place = (t * heads + n) * HS
                sent[a, :, place : place + HS] = one.astype(BF16)
            if b in sends:
                first, last = sends[b]
                at_s = pl.ds(first * HS, (last - first) * HS)
                for to in partners:
                    pltpu.make_async_remote_copy(
                        src_ref=sent.at[a, pl.ds(pl.multiple_of(to * chunk, 16), chunk), at_s],
                        dst_ref=got.at[a, own, at_s],
                        send_sem=in_send.at[a],
                        recv_sem=in_recv.at[a],
                        device_id=(to, head),
                        device_id_type=MESH,
                    ).start()
        copy = pltpu.make_async_copy(sent.at[a, own, :], got.at[a, own, :], load_sem.at[9 + a])
        copy.start()
        in_local.append(copy)

    per_part = part // 16
    for a in range(2):
        for q in (2 * a, 2 * a + 1):
            lat_loads[q].wait()
            lax.fori_loop(q * per_part, (q + 1) * per_part, normalise, 0)
        project(a)

    per_slot = positions // slots // 2
    row_at = lax.broadcasted_iota(jnp.int32, (8, side), 0)
    col_at = lax.broadcasted_iota(jnp.int32, (8, side), 1)
    bias = jnp.where(row_at % per_slot == col_at % per_slot, 0.0, -1e9).astype(F32)
    own_cols = pl.ds(pl.multiple_of(y * cols, 128), cols)
    before = (me + slots - 1) % slots

    def attend(a):
        in_local[a].wait()
        others = got.at[a, pl.ds(0, side - chunk), :]
        pltpu.make_async_copy(others, others, in_recv.at[a]).wait()
        for n in range(heads):
            keys, values, queries = (
                got[a, :, (t * heads + n) * HS : (t * heads + n + 1) * HS] for t in range(3)
            )
            values = jnp.concatenate([values, jnp.ones((side, HS), BF16)], axis=1)
            scores = lax.dot_general(
                queries, keys, (((1,), (1,)), ((), ())), preferred_element_type=F32
            )
            scores = scores.reshape(side // 8, 8, side) + bias[None]
            largest = jnp.max(scores, axis=-1, keepdims=True)
            powers = jnp.exp((scores - largest) * (1.0 / HS**0.5))
            mixed = jnp.dot(
                powers.reshape(side, side).astype(BF16), values, preferred_element_type=F32
            )
            attended[a * side : (a + 1) * side, n * HS : (n + 1) * HS] = (
                mixed[:, :HS] / mixed[:, HS:]
            ).astype(BF16)

        arrive = gathered.at[pl.ds(pl.multiple_of(a * side + me * chunk, 16), chunk), own_cols]
        sem = back_recv.at[a * 2 + me // (slots // 2)]
        for to in partners:
            owner = (to + slots - 1) % slots
            pltpu.make_async_remote_copy(
                src_ref=attended.at[pl.ds(pl.multiple_of(a * side + owner * chunk, 16), chunk), :],
                dst_ref=arrive,
                send_sem=back_send.at[a],
                recv_sem=sem,
                device_id=(to, head),
                device_id_type=MESH,
            ).start()
        pltpu.make_async_copy(
            attended.at[pl.ds(pl.multiple_of(a * side + before * chunk, 16), chunk), :],
            arrive,
            sem,
        ).start()

    def y_copy(r, kind, steps, source, start, count):
        piece = gathered.at[
            pl.ds(r * quarter + start, count), pl.ds(pl.multiple_of(source * cols, 128), cols)
        ]
        copy = pltpu.make_async_remote_copy(
            src_ref=piece,
            dst_ref=piece,
            send_sem=y_send.at[r, kind],
            recv_sem=y_recv.at[r, kind],
            device_id=ring(steps),
            device_id_type=MESH,
        )
        copy.start()
        return copy

    y_first, y_second = {}, {}

    def spread(r):
        piece = gathered.at[pl.ds(r * quarter, quarter), own_cols]
        pltpu.make_async_copy(piece, piece, back_recv.at[r]).wait()
        y_first[r] = (y_copy(r, 0, 1, y, 0, quarter), y_copy(r, 1, ys - 1, y, 0, quarter))

    def forward(r):
        low, high = y_first[r]
        low.wait()
        one = y_copy(r, 2, 1, (y + ys - 1) % ys, 0, quarter // 2)
        high.wait()
        two = y_copy(r, 3, ys - 1, (y + 1) % ys, quarter // 2, quarter // 2)
        y_second[r] = (one, two)

    x_copies = []

    def combine(r):
        at_r = slice(r * quarter, (r + 1) * quarter)
        for copy in y_second[r]:
            copy.wait()
        partial = jnp.dot(gathered[at_r, :], wout[...], preferred_element_type=F32)
        lower, upper = partial[:, :out_cols], partial[:, out_cols:]
        psend[at_r, :] = jnp.where(xlo == 0, upper, lower).astype(BF16)
        copy = pltpu.make_async_remote_copy(
            src_ref=psend.at[pl.ds(r * quarter, quarter), :],
            dst_ref=precv.at[pl.ds(r * quarter, quarter), :],
            send_sem=x_send.at[r],
            recv_sem=x_recv.at[r],
            device_id=(me, y * 2 + 1 - xlo),
            device_id_type=MESH,
        )
        copy.start()
        x_copies.append(copy)
        pown[at_r, :] = jnp.where(xlo == 0, lower, upper)

    def finish(r):
        x_copies[r].wait()
        for j in range(r * quarter // 64, (r + 1) * quarter // 64):
            at = slice(j * 16, (j + 1) * 16)
            total = pown[j * 64 : (j + 1) * 64, :] + precv[j * 64 : (j + 1) * 64, :].astype(F32)
            moved = [[None, None] for _ in range(frames)]
            for v in range(2):
                for u in range(2):
                    start = v * 32 + u * 8
                    moved[2 * u][v], moved[2 * u + 1][v] = swap_halves(
                        total[start : start + 8], total[start + 16 : start + 24]
                    )
            for f in range(frames):
                added = jnp.concatenate([moved[f][0] * gate_in[f], moved[f][1] * gate_in[f]], axis=0)
                out_ref[f, at, :] = (residual[f, at, :].astype(F32) + added).astype(BF16)

    attend(0)
    spread(0)
    spread(1)
    attend(1)

    sib_copies = []
    for k, copy in w_copies:
        copy.wait()
        source = (y + ys - k) % ys
        piece = wout.at[pl.ds(pl.multiple_of(source * cols + core * half, 64), half), :]
        passed = pltpu.make_async_remote_copy(
            src_ref=piece,
            dst_ref=piece,
            send_sem=sib_send.at[k - 1],
            recv_sem=sib_recv.at[k - 1],
            device_id=(sibling, head),
            device_id_type=MESH,
        )
        passed.start()
        sib_copies.append(passed)

    forward(0)
    forward(1)
    spread(2)
    spread(3)
    for copy in [own_w] + sib_copies:
        copy.wait()
    combine(0)
    forward(2)
    combine(1)
    forward(3)
    combine(2)
    combine(3)
    for copy in shift_copies:
        copy.wait()
    for r in range(4):
        finish(r)

    for a in range(2):
        others = sent.at[a, pl.ds(0, side - chunk), :]
        pltpu.make_async_copy(others, others, in_send.at[a]).wait()
        others = attended.at[pl.ds(0, side - chunk), :]
        pltpu.make_async_copy(others, others, back_send.at[a]).wait()


def on_device(slots, ys, latents, levels, mod_table, wq, wk, wv, wo, qgain, kgain):
    frames, positions, width = latents.shape
    cols = wq.shape[1]
    rows = frames * positions
    out_cols = width // (2 * ys)
    vmem = pl.BlockSpec(memory_space=pltpu.VMEM)
    hbm = pl.BlockSpec(memory_space=pl.ANY)
    dma = pltpu.SemaphoreType.DMA
    return pl.pallas_call(
        functools.partial(block_kernel, slots, ys),
        out_shape=jax.ShapeDtypeStruct((frames, positions, out_cols), BF16),
        in_specs=[pl.BlockSpec(memory_space=pltpu.SMEM)] + [hbm] * 6 + [vmem] * 2,
        out_specs=vmem,
        scratch_shapes=[
            pltpu.VMEM((frames, positions, width), BF16),
            pltpu.VMEM((3, mod_table.shape[0], width), F32),
            pltpu.VMEM((frames, 2, 8, width), F32),
            pltpu.VMEM((rows, width), BF16),
            pltpu.VMEM((3, width, cols), BF16),
            pltpu.VMEM((2, rows // 2, 3 * cols), BF16),
            pltpu.VMEM((2, rows // 2, 3 * cols), BF16),
            pltpu.VMEM((rows, cols), BF16),
            pltpu.VMEM((rows, ys * cols), BF16),
            pltpu.VMEM((ys * cols, 2 * out_cols), BF16),
            pltpu.VMEM((rows, out_cols), BF16),
            pltpu.VMEM((rows, out_cols), BF16),
            pltpu.VMEM((rows, out_cols), F32),
            pltpu.VMEM((frames, positions, out_cols), BF16),
            pltpu.VMEM((frames, 8, out_cols), F32),
            pltpu.VMEM((frames, 8, out_cols), F32),
            dma((11,)),
            dma((2,)),
            dma((2,)),
            dma((2,)),
            dma((4,)),
            dma((4, 4)),
            dma((4, 4)),
            dma((ys - 1,)),
            dma((ys - 1,)),
            dma((ys - 1,)),
            dma((ys - 1,)),
            dma((4,)),
            dma((4,)),
            dma((2,)),
            dma((2,)),
        ],
        compiler_params=pltpu.CompilerParams(
            collective_id=0, has_side_effects=True, vmem_limit_bytes=60 << 20
        ),
        name="temporal_block",
    )(levels, latents, jnp.transpose(mod_table, (1, 0, 2)), wq, wk, wv, wo, qgain, kgain)


def solution(mesh):
    return jax.shard_map(
        functools.partial(on_device, mesh.shape["frame"], mesh.shape["head"] // 2),
        mesh=mesh,
        in_specs=(
            P("frame", None, None),
            P("frame"),
            P(),
            P(None, "head"),
            P(None, "head"),
            P(None, "head"),
            P("head", None),
            P("head"),
            P("head"),
        ),
        out_specs=P("frame", None, "head"),
        check_vma=False,
    )
```
